32 devices in a mesh: row: 4 (over y, core), col: 8 (over z, x).
Axes of the slice: x: 2, y: 2, z: 4, core: 2. Of those that a mesh axis runs over, the one named last changes fastest.
Arguments:
- layer_input: bfloat16 [256, 12288], P('col', 'row'), may hold values from -0.375 to 0.375
- weight: bfloat16 [12288, 49152], P('row', 'col'), may hold values from -0.0546875 to 0.0546875
- hidden_pre: bfloat16 [256, 49152], P('row', 'col'), may hold values from -8 to 8
- upstream: bfloat16 [256, 49152], P('row', 'col'), may hold values from -6 to 6
Outputs:
- input_grad: bfloat16 [256, 12288], P('col', 'row')
- weight_grad: bfloat16 [12288, 49152], P('row', 'col')
The draws below stay inside these ranges and needn't reach their ends.
All inputs are finite; a program needn't handle non-finite values.
Results may differ from the reference program's by a relative error of at most 0.005.
Values may be sent and summed in bfloat16 or wider, within the bound.
No kernel may reach another device: no remote copies, remote signals or barrier semaphores. Data moves between devices by JAX's collectives and lax.ppermute only.
A program may use at most 256 MiB of HBM per device.

```python
import jax
import jax.numpy as jnp
from jax import lax

D = 12288
FF = 49152
TOKENS = 256


def with_spikes(array, stream_key, source, target, blocks, factor):
    def block_of(axis_at):
        return (jnp.arange(array.shape[axis_at]) // (array.shape[axis_at] // blocks)).reshape((-1,) + (1,) * (array.ndim - 1 - axis_at))

    first = jax.random.permutation(stream_key, blocks)[block_of(target)]
    other_side = (block_of(target) + blocks // 2) % blocks
    return jnp.where((block_of(source) == first) | (block_of(source) == other_side), factor * array, array)


def steps_of(own_key, dims, shards, smallest, top_value):
    level = 1.0
    for position, shards_of in shards:
        draws = jax.random.uniform(jax.random.fold_in(jax.random.fold_in(own_key, 6), position), (shards_of,), jnp.float32, smallest / len(shards), top_value / len(shards))
        level = level * jnp.repeat(jnp.exp(draws), dims[position] // shards_of).reshape((-1,) + (1,) * (len(dims) - 1 - position))
    return level


def noise(own_key, dims, spread, reach, shards=(), kind=jnp.bfloat16):
    level = steps_of(own_key, dims, shards, -0.22, 0.18) if shards else 1.0
    values = jax.random.normal(own_key, dims, jnp.float32) * spread * level
    return jnp.minimum(jnp.maximum(values, -reach), reach).astype(kind)


def gaussian_with(rng, extent, spread, most, cuts, heavy, kind=jnp.bfloat16):
    drawn = spread * jax.random.normal(rng, extent, jnp.float32)
    if cuts:
        drawn = drawn * steps_of(rng, extent, cuts, -0.22, 0.18)
    return jnp.clip(with_spikes(drawn, jax.random.fold_in(rng, 3), *heavy), -most, most).astype(kind)


def setup_inputs(seed: int = 0) -> dict:
    arg_keys = jax.random.split(jax.random.key(seed), 5)
    layer_input = noise(arg_keys[0], (TOKENS, D), (TOKENS ** -0.5), 0.375, ((0, 8), (1, 4)))
    weight = noise(arg_keys[1], (D, FF), D ** -0.5, 0.0546875, ((0, 4), (1, 8)))
    hidden_pre = noise(arg_keys[2], (TOKENS, FF), 1.5, 8.0, ((0, 4), (1, 8)))
    upstream = gaussian_with(arg_keys[3], (TOKENS, FF), 1.0, 6.0, ((0, 4), (1, 8)), (1, 0, 8, 2.0))
    return dict(layer_input=layer_input, weight=weight, hidden_pre=hidden_pre, upstream=upstream)


def gelu_slope(value):
    coeff = 0.7978845608028654
    inner = coeff * (value + 0.044715 * value * value * value)
    tanh_val = jnp.tanh(inner)
    return 0.5 * (1.0 + tanh_val) + 0.5 * value * (1.0 - tanh_val * tanh_val) * coeff * (1.0 + 3.0 * 0.044715 * value * value)


def reference(layer_input, weight, hidden_pre, upstream):
    slope = gelu_slope(hidden_pre.astype(jnp.float32))
    hidden_grad = (upstream.astype(jnp.float32) * slope).astype(jnp.bfloat16)
    input_grad = lax.dot_general(hidden_grad, weight, (((1,), (1,)), ((), ())), preferred_element_type=jnp.float32).astype(jnp.bfloat16)
    weight_grad = lax.dot_general(layer_input, hidden_grad, (((0,), (0,)), ((), ())), preferred_element_type=jnp.float32).astype(jnp.bfloat16)
    return input_grad, weight_grad
```

```python
import functools

import jax
import jax.numpy as jnp
from jax import lax
from jax.experimental import pallas as pl
from jax.experimental.pallas import tpu as pltpu
from jax.sharding import PartitionSpec as P

TERMS_SCALE = 1
OUTER_SCALE = 1


def gelu_slope(value):
    coeff = 0.7978845608028654
    inner = coeff * (value + 0.044715 * value * value * value)
    tanh_val = jnp.tanh(inner)
    return 0.5 * (1.0 + tanh_val) + 0.5 * value * (1.0 - tanh_val * tanh_val) * coeff * (
        1.0 + 3.0 * 0.044715 * value * value
    )


def hidden_grad_of(pre, upstream):
    return (upstream.astype(jnp.float32) * gelu_slope(pre.astype(jnp.float32))).astype(jnp.bfloat16)


def grad_rows(hidden_rows, weight):
    return lax.dot_general(
        hidden_rows, weight, (((1,), (1,)), ((), ())), preferred_element_type=jnp.float32
    )


def outer_sum(input_rows, hidden_rows):
    return lax.dot_general(
        input_rows, hidden_rows, (((0,), (0,)), ((), ())), preferred_element_type=jnp.float32
    )


def general_shards(layer_input, weight, hidden_pre, upstream):
    hidden_grad = hidden_grad_of(hidden_pre, upstream)
    hidden_all = lax.all_gather(hidden_grad, "row", axis=0, tiled=True)
    input_all = lax.all_gather(layer_input, "col", axis=0, tiled=True)
    terms = grad_rows(hidden_all, weight)
    input_sum = lax.psum_scatter(terms, "col", scatter_dimension=0, tiled=True)
    weight_sum = outer_sum(input_all, hidden_all)
    return (input_sum.astype(jnp.bfloat16), weight_sum.astype(jnp.bfloat16))


def slope_columns(pre, up, start, size, out):
    step = 512

    @pl.loop(0, size // step)
    def _(i):
        here = pl.ds(pl.multiple_of(start + i * step, step), step)
        out[:, pl.ds(pl.multiple_of(i * step, step), step)] = hidden_grad_of(pre[:, here], up[:, here])


def first_hidden_kernel(size, pre_hbm, up_hbm, pre, up, out, sems):
    copies = []
    for n, cols in enumerate((pl.ds(0, size), pl.ds(size, pre.shape[1] - size))):
        for m, (source, target) in enumerate(((pre_hbm, pre), (up_hbm, up))):
            copies.append(pltpu.make_async_copy(source.at[:, cols], target.at[:, cols], sems.at[n, m]))
            copies[-1].start()
    copies[0].wait()
    copies[1].wait()
    slope_columns(pre, up, 0, size, out)
    copies[2].wait()
    copies[3].wait()


def first_hidden(pre, up, size):
    rows, width = pre.shape
    vmem, hbm = pl.BlockSpec(memory_space=pltpu.VMEM), pl.BlockSpec(memory_space=pl.ANY)
    return pl.pallas_call(
        functools.partial(first_hidden_kernel, size),
        in_specs=[hbm] * 2,
        out_specs=[vmem] * 3,
        out_shape=[pltpu.VMEM(shape, jnp.bfloat16) for shape in ((rows, width), (rows, width), (rows, size))],
        scratch_shapes=[pltpu.SemaphoreType.DMA((2, 2))],
        compiler_params=pltpu.CompilerParams(vmem_limit_bytes=8 << 20),
        cost_estimate=pl.CostEstimate(flops=0, bytes_accessed=4 * pre.size, transcendentals=0),
        name="first_hidden",
    )(pre, up)


def next_hidden_kernel(start, size, pre, up, before, out):
    slope_columns(pre, up, start, size, out)


def next_hidden(pre, up, before, start, size):
    rows = pre.shape[0]
    vmem, hbm = pl.BlockSpec(memory_space=pltpu.VMEM), pl.BlockSpec(memory_space=pl.ANY)
    return pl.pallas_call(
        functools.partial(next_hidden_kernel, start, size),
        in_specs=[vmem, vmem, hbm],
        out_specs=vmem,
        out_shape=pltpu.VMEM((rows, size), jnp.bfloat16),
        compiler_params=pltpu.CompilerParams(vmem_limit_bytes=8 << 20),
        cost_estimate=pl.CostEstimate(flops=0, bytes_accessed=rows * size, transcendentals=0),
        name="next_hidden",
    )(pre, up, before)


def joined_kernel(*refs):
    parts, out = refs[:-1], refs[-1]
    start = 0
    for part in parts:
        out[:, pl.ds(start, part.shape[1])] = part[...]
        start += part.shape[1]


def joined(parts):
    rows, width = parts[0].shape[0], sum(part.shape[1] for part in parts)
    vmem = pl.BlockSpec(memory_space=pltpu.VMEM)
    return pl.pallas_call(
        joined_kernel,
        in_specs=[vmem] * len(parts),
        out_specs=vmem,
        out_shape=pltpu.VMEM((rows, width), jnp.bfloat16),
        compiler_params=pltpu.CompilerParams(vmem_limit_bytes=8 << 20),
        cost_estimate=pl.CostEstimate(flops=0, bytes_accessed=rows * width, transcendentals=0),
        name="joined",
    )(*parts)


def weight_copies(weight_ref, tiles, sems, start, size, count):
    rows = weight_ref.shape[0] // count
    return [
        pltpu.make_async_copy(
            weight_ref.at[pl.ds(n * rows, rows), pl.ds(start, size)], tiles.at[pl.ds(n * rows, rows)], sems.at[n]
        )
        for n in range(count)
    ]


COPIES = 6


def load_kernel(start, size, weight_ref, input_ref, after_ref, tiles, input_copy, sems):
    copies = weight_copies(weight_ref, tiles, sems, start, size, COPIES)
    copies.append(pltpu.make_async_copy(input_ref, input_copy, sems.at[COPIES]))
    for copy in copies:
        copy.start()
    for copy in copies:
        copy.wait()


def load_part(weight, layer_input, after, start, size):
    model = weight.shape[0]
    hbm = pl.BlockSpec(memory_space=pl.ANY)
    return pl.pallas_call(
        functools.partial(load_kernel, start, size),
        in_specs=[hbm] * 3,
        out_specs=[pl.BlockSpec(memory_space=pltpu.VMEM)] * 2,
        out_shape=[pltpu.VMEM((model, size), jnp.bfloat16), pltpu.VMEM(layer_input.shape, jnp.bfloat16)],
        scratch_shapes=[pltpu.SemaphoreType.DMA((COPIES + 1,))],
        compiler_params=pltpu.CompilerParams(vmem_limit_bytes=16 << 20),
        cost_estimate=pl.CostEstimate(flops=0, bytes_accessed=2 * size * model, transcendentals=0),
        name="weight_load",
    )(weight, layer_input, after)


def gather_hidden(place_ref, own, sib, far, start, hidden):
    _, rows, size = far.shape
    cols, core = pl.ds(start, size), place_ref[3]
    for j, part in enumerate((own.at[:, cols], sib.at[:, cols], far.at[core], far.at[1 - core])):
        hidden[pl.ds(rows * j, rows)] = part[...]


def terms_kernel(starts, sizes, n, block, place_ref, own, sib, far, tiles, *refs):
    first, last = n == 0, n == len(sizes) - 1
    refs = list(refs)
    held = None if first else refs.pop(0)
    weight = None if last else refs.pop(0)
    if last:
        sends, keeps, refs = refs[:4], refs[4:8], refs[8:]
        total, hidden = refs
    else:
        total, later, hidden, sems = refs
        copies = weight_copies(weight, later, sems, starts[n + 1], sizes[n + 1], COPIES)
        for copy in copies:
            copy.start()
    gather_hidden(place_ref, own, sib, far, starts[n], hidden)
    rows, model = far.shape[1], tiles.shape[0]

    @pl.loop(0, model // block)
    def _(i):
        here = pl.ds(pl.multiple_of(i * block, block), block)
        term = grad_rows(hidden[...], tiles[here]).reshape(8, rows // 2, block)
        if not first:
            term = term + held[:, :, here]
        total[:, :, here] = term

    if last:
        row, z, x = place_ref[0], place_ref[1], place_ref[2]
        for k in range(4):
            slot = 2 * (row ^ z ^ k)
            sends[k][...] = total[slot + (1 - x)].astype(jnp.bfloat16)
            keeps[k][...] = total[slot + x]
    else:
        for copy in copies:
            copy.wait()


def terms_part(place, parts, tiles, held, weight, starts, sizes, n):
    _, rows, size = parts[2].shape
    model = weight.shape[0]
    block = 1024
    vmem, hbm = pl.BlockSpec(memory_space=pltpu.VMEM), pl.BlockSpec(memory_space=pl.ANY)
    first, last = n == 0, n == len(sizes) - 1
    half = rows // 2
    operands = [place, *parts, tiles]
    in_specs = [pl.BlockSpec(memory_space=pltpu.SMEM)] + [vmem] * 4
    aliases = {}
    if not first:
        if not last:
            aliases = {len(operands): 0}
        operands.append(held)
        in_specs.append(vmem)
    if not last:
        operands.append(weight)
        in_specs.append(hbm)
    scratch = [pltpu.VMEM((4 * rows, size), jnp.bfloat16)]
    if last:
        scratch = [pltpu.VMEM((8, half, model), jnp.float32)] + scratch
        out_shape = [pltpu.VMEM((half, model), jnp.bfloat16)] * 4
        out_shape += [pltpu.VMEM((half, model), jnp.float32)] * 4
    else:
        scratch.append(pltpu.SemaphoreType.DMA((COPIES,)))
        out_shape = [
            pltpu.VMEM((8, half, model), jnp.float32),
            pltpu.VMEM((model, sizes[n + 1]), jnp.bfloat16),
        ]
    return pl.pallas_call(
        functools.partial(terms_kernel, starts, sizes, n, block),
        in_specs=in_specs,
        out_specs=[vmem] * len(out_shape),
        out_shape=out_shape,
        scratch_shapes=scratch,
        input_output_aliases=aliases,
        compiler_params=pltpu.CompilerParams(vmem_limit_bytes=16 << 20),
        cost_estimate=pl.CostEstimate(flops=8 * rows * size * model, bytes_accessed=TERMS_SCALE * 2 * size * model, transcendentals=0),
        name="terms",
    )(*operands)


def input_kernel(place_ref, *refs):
    blocks, out, held = refs[:8], refs[8], refs[9]
    row, z, x = place_ref[0], place_ref[1], place_ref[2]
    half = blocks[0].shape[0]
    for k in range(4):
        for i in range(2):
            held[2 * (row ^ z ^ k) + (x ^ i)] = blocks[2 * k + i][...]
    out[...] = held[...].reshape(8 * half, -1).T


def input_columns(place, blocks):
    half, model = blocks[0].shape
    vmem = pl.BlockSpec(memory_space=pltpu.VMEM)
    return pl.pallas_call(
        input_kernel,
        in_specs=[pl.BlockSpec(memory_space=pltpu.SMEM)] + [vmem] * 8,
        out_specs=vmem,
        out_shape=pltpu.VMEM((model, 8 * half), jnp.bfloat16),
        scratch_shapes=[pltpu.VMEM((8, half, model), jnp.bfloat16)],
        compiler_params=pltpu.CompilerParams(vmem_limit_bytes=16 << 20),
        cost_estimate=pl.CostEstimate(flops=0, bytes_accessed=32 * half * model, transcendentals=0),
        name="input_columns",
    )(place, *blocks)


def outer_kernel(start, size, block, first, place_ref, columns_ref, own, sib, far, *refs):
    out, hidden, tiles, sems = refs if first else refs[1:]
    gather_hidden(place_ref, own, sib, far, start, hidden)
    slots = tiles.shape[0]
    copies = []
    for n in range(size // block):
        slot = n % slots
        if n >= slots:
            copies[n - slots].wait()
        tiles[slot] = jnp.dot(
            columns_ref[...], hidden[:, pl.ds(n * block, block)], preferred_element_type=jnp.float32
        ).astype(jnp.bfloat16)
        copies.append(
            pltpu.make_async_copy(tiles.at[slot], out.at[:, pl.ds(start + n * block, block)], sems.at[slot])
        )
        copies[-1].start()
    for copy in copies[-slots:]:
        copy.wait()


def outer_part(place, columns, parts, held, start, whole):
    _, rows, size = parts[2].shape
    model, tokens = columns.shape
    block = 512
    first = held is None
    vmem, hbm = pl.BlockSpec(memory_space=pltpu.VMEM), pl.BlockSpec(memory_space=pl.ANY)
    operands = [place, columns, *parts] + ([] if first else [held])
    slots = min(3, size // block)
    return pl.pallas_call(
        functools.partial(outer_kernel, start, size, block, first),
        in_specs=[pl.BlockSpec(memory_space=pltpu.SMEM)] + [vmem] * 4 + ([] if first else [hbm]),
        out_specs=hbm,
        out_shape=jax.ShapeDtypeStruct((model, whole), jnp.bfloat16),
        scratch_shapes=[
            pltpu.VMEM((tokens, size), jnp.bfloat16),
            pltpu.VMEM((slots, model, block), jnp.bfloat16),
            pltpu.SemaphoreType.DMA((slots,)),
        ],
        input_output_aliases={} if first else {5: 0},
        compiler_params=pltpu.CompilerParams(vmem_limit_bytes=16 << 20),
        cost_estimate=pl.CostEstimate(
            flops=2 * tokens * size * model, bytes_accessed=OUTER_SCALE * 2 * size * model, transcendentals=0
        ),
        name="outer",
    )(*operands)


def fenced(value, other):
    return lax.optimization_barrier((value, other))[0]


def swap(value, axis, size, bits):
    return lax.ppermute(value, axis, [(n, n ^ bits) for n in range(size)])


def paired_shards(layer_input, weight, hidden_pre, upstream):
    hidden = hidden_pre.shape[1]
    parts = 3
    sizes = [hidden // parts] * parts
    starts = [sum(sizes[:n]) for n in range(parts)]
    row, col = lax.axis_index("row"), lax.axis_index("col")
    place = jnp.stack([row, col // 2, col % 2, row % 2]).astype(jnp.int32)

    across = functools.partial(swap, axis="col", size=8)
    along = functools.partial(swap, axis="row", size=4)

    pre, up, part = first_hidden(hidden_pre, upstream, sizes[0])
    sent = [part]
    for n in range(1, parts):
        sent.append(next_hidden(pre, up, sent[-1], starts[n], sizes[n]))
    far = [along(sent[0], bits=2)]
    own = joined(sent)
    sib = along(own, bits=1)

    far.append(along(fenced(sent[1], sib), bits=2))
    early = fenced(layer_input, sib)
    lines = [layer_input, None, across(early, bits=4), across(early, bits=6)]
    crossed = [across(early, bits=1)]
    tiles, _ = load_part(weight, layer_input, sib, starts[0], sizes[0])
    far.append(along(fenced(sent[2], tiles), bits=2))
    tiles = fenced(tiles, crossed[0])

    pairs, held = [], None
    for n in range(parts):
        far[n], tiles, held = lax.optimization_barrier((far[n], tiles, held))
        pairs.append(lax.all_gather(far[n], "row", axis=0, axis_index_groups=[[0, 1], [2, 3]]))
        out = terms_part(place, [own, sib, pairs[n]], tiles, held, weight, starts, sizes, n)
        if n < parts - 1:
            held, tiles = out
        if n == 0:
            lines[1] = across(fenced(layer_input, tiles), bits=2)
            crossed.append(across(fenced(lines[3], tiles), bits=1))
        if n == 1:
            for k in (2, 1):
                crossed.append(across(fenced(lines[k], tiles), bits=1))
    sends, keeps = out[:4], out[4:]
    blocks = []
    for k, n in enumerate((0, 3, 2, 1)):
        blocks += [lines[k], crossed[n]]

    order = (2, 3, 1, 0)
    got = {k: across(sends[k], bits=1) for k in order}
    columns = input_columns(place, blocks)
    weight_grad, ends, pair = None, {}, {}
    for n, k in enumerate(order):
        if n < parts:
            weight_grad = outer_part(place, columns, [own, sib, pairs[n]], weight_grad, starts[n], hidden)
        if k:
            got[k], weight_grad = lax.optimization_barrier((got[k], weight_grad))
        pair[k] = keeps[k] + got[k].astype(jnp.float32)
        if k:
            rounded = pair[k].astype(jnp.bfloat16)
            rounded, columns = lax.optimization_barrier((rounded, columns))
            ends[k] = across(rounded, bits=2 * k)
    input_sum = pair[0]
    for n, k in enumerate(order[:3]):
        input_sum = input_sum + ends[k].astype(jnp.float32)
        if n < 2:
            input_sum, ends[order[n + 1]] = lax.optimization_barrier((input_sum, ends[order[n + 1]]))
    return (input_sum.astype(jnp.bfloat16), weight_grad)


def solution(mesh):
    in_specs = (P("col", "row"), P("row", "col"), P("row", "col"), P("row", "col"))
    out_specs = (P("col", "row"), P("row", "col"))
    paired = mesh.shape["row"] == 4 and mesh.shape["col"] == 8
    shards = paired_shards if paired else general_shards
    return jax.shard_map(shards, mesh=mesh, in_specs=in_specs, out_specs=out_specs, check_vma=False)
```

```python
import functools

import jax
import jax.numpy as jnp
from jax import lax
from jax.experimental import pallas as pl
from jax.experimental.pallas import tpu as pltpu
from jax.sharding import PartitionSpec as P

COPIES = 6
VMEM = pl.BlockSpec(memory_space=pltpu.VMEM)
HBM = pl.BlockSpec(memory_space=pltpu.HBM)
SMEM = pl.BlockSpec(memory_space=pltpu.SMEM)
CORES = [[0, 1], [2, 3]]


def gelu_slope(value):
    coeff = 0.7978845608028654
    inner = coeff * (value + 0.044715 * value * value * value)
    tanh_val = jnp.tanh(inner)
    return 0.5 * (1.0 + tanh_val) + 0.5 * value * (1.0 - tanh_val * tanh_val) * coeff * (
        1.0 + 3.0 * 0.044715 * value * value
    )


def hidden_grad_of(pre, upstream):
    return (upstream.astype(jnp.float32) * gelu_slope(pre.astype(jnp.float32))).astype(jnp.bfloat16)


def grad_rows(hidden_rows, weight):
    return lax.dot_general(
        hidden_rows, weight, (((1,), (1,)), ((), ())), preferred_element_type=jnp.float32
    )


def outer_sum(input_rows, hidden_rows):
    return lax.dot_general(
        input_rows, hidden_rows, (((0,), (0,)), ((), ())), preferred_element_type=jnp.float32
    )


def general_shards(layer_input, weight, hidden_pre, upstream):
    hidden_grad = hidden_grad_of(hidden_pre, upstream)
    hidden_all = lax.all_gather(hidden_grad, "row", axis=0, tiled=True)
    input_all = lax.all_gather(layer_input, "col", axis=0, tiled=True)
    terms = grad_rows(hidden_all, weight)
    input_sum = lax.psum_scatter(terms, "col", scatter_dimension=0, tiled=True)
    weight_sum = outer_sum(input_all, hidden_all)
    return (input_sum.astype(jnp.bfloat16), weight_sum.astype(jnp.bfloat16))


def slope_columns(pre, up, start, size, outs):
    step = 512

    @pl.loop(0, size // step)
    def _(i):
        here = pl.ds(pl.multiple_of(start + i * step, step), step)
        value = hidden_grad_of(pre[:, here], up[:, here])
        for out, first in outs:
            out[:, pl.ds(pl.multiple_of(first + i * step, step), step)] = value


def hidden_kernel(starts, sizes, pre_hbm, up_hbm, *refs):
    parts, refs = refs[: len(sizes)], refs[len(sizes) :]
    own, pre, up, sems = refs
    copies = []
    for n, (start, size) in enumerate(zip(starts, sizes)):
        cols = pl.ds(start, size)
        for m, (source, target) in enumerate(((pre_hbm, pre), (up_hbm, up))):
            copies.append(pltpu.make_async_copy(source.at[:, cols], target.at[:, cols], sems.at[n, m]))
            copies[-1].start()
    for n, (part, start, size) in enumerate(zip(parts, starts, sizes)):
        copies[2 * n].wait()
        copies[2 * n + 1].wait()
        slope_columns(pre, up, start, size, [(part, 0), (own, start)])


def hidden_parts(pre, up, starts, sizes):
    rows, width = pre.shape
    outs = [(rows, size) for size in sizes] + [(rows, width)]
    return pl.pallas_call(
        functools.partial(hidden_kernel, starts, sizes),
        in_specs=[HBM] * 2,
        out_specs=[VMEM] * len(outs),
        out_shape=[pltpu.VMEM(shape, jnp.bfloat16) for shape in outs],
        scratch_shapes=[
            pltpu.VMEM((rows, width), jnp.bfloat16),
            pltpu.VMEM((rows, width), jnp.bfloat16),
            pltpu.SemaphoreType.DMA((len(sizes), 2)),
        ],
        compiler_params=pltpu.CompilerParams(vmem_limit_bytes=60 << 20),
        cost_estimate=pl.CostEstimate(flops=20 * pre.size, bytes_accessed=6 * pre.size, transcendentals=pre.size),
        name="hidden_grad",
    )(pre, up)


def weight_copies(weight, tiles, sems, start, size):
    rows = weight.shape[0] // COPIES
    return [
        pltpu.make_async_copy(
            weight.at[pl.ds(n * rows, rows), pl.ds(start, size)], tiles.at[pl.ds(n * rows, rows)], sems.at[n]
        )
        for n in range(COPIES)
    ]


def pair_kernel(first, second, out):
    out[0] = first[...]
    out[1] = second[...]


def pair_of(first, second):
    return pl.pallas_call(
        pair_kernel,
        in_specs=[VMEM] * 2,
        out_specs=VMEM,
        out_shape=pltpu.VMEM((2, *first.shape), first.dtype),
        compiler_params=pltpu.CompilerParams(vmem_limit_bytes=16 << 20),
        cost_estimate=pl.CostEstimate(flops=0, bytes_accessed=8 * first.size, transcendentals=0),
        name="pair",
    )(first, second)


def gather_hidden(place_ref, own, sib, far, start, offset, hidden):
    rows, size = own.shape[0], hidden.shape[1]
    cols, here, core = pl.ds(start + offset, size), pl.ds(offset, size), place_ref[3]
    for j, part in enumerate((own.at[:, cols], sib.at[:, cols], far.at[core, :, here], far.at[1 - core, :, here])):
        hidden[pl.ds(rows * j, rows)] = part[...]


def terms_kernel(starts, n, first, last, place_ref, own, sib, far, weight, *refs):
    held, refs = (None, refs) if first else (refs[0], refs[1:])
    if last:
        sends, keeps, refs = refs[:3], refs[3:7], refs[7:]
        total, hidden, tiles, sems = refs
    else:
        total, token, hidden, tiles, sems = refs
        token[...] = jnp.zeros_like(token)
    copies = weight_copies(weight, tiles, sems, starts[n], tiles.shape[1])
    for copy in copies:
        copy.start()
    gather_hidden(place_ref, own, sib, far, starts[n], 0, hidden)
    rows, model = own.shape[0], tiles.shape[0]
    block = model // COPIES
    for i, copy in enumerate(copies):
        copy.wait()
        here = pl.ds(i * block, block)
        term = grad_rows(hidden[...], tiles[here]).reshape(8, rows // 2, block)
        total[:, :, here] = term if first else term + held[:, :, here]

    if last:
        row, z, x = place_ref[0], place_ref[1], place_ref[2]
        slots = [2 * (row ^ z ^ k) for k in range(4)]
        sends[0][0] = total[slots[1] + x].astype(jnp.bfloat16)
        sends[0][1] = total[slots[1] + (1 - x)].astype(jnp.bfloat16)
        for k in (2, 3):
            sends[k - 1][...] = total[slots[k] + (1 - x)].astype(jnp.bfloat16)
            keeps[k][...] = total[slots[k] + x]
        keeps[0][...] = total[slots[0] + x]
        keeps[1][...] = total[slots[0] + (1 - x)]


def terms_part(place, parts, weight, held, starts, sizes, n):
    _, rows, size = parts[2].shape
    model = weight.shape[0]
    first, last = n == 0, n == len(sizes) - 1
    half = rows // 2
    operands = [place, *parts, weight]
    in_specs = [SMEM] + [VMEM] * 3 + [HBM]
    aliases = {}
    if not first:
        if not last:
            aliases[len(operands)] = 0
        operands.append(held)
        in_specs.append(VMEM)
    scratch = [
        pltpu.VMEM((4 * rows, size), jnp.bfloat16),
        pltpu.VMEM((model, size), jnp.bfloat16),
        pltpu.SemaphoreType.DMA((COPIES,)),
    ]
    if last:
        scratch = [pltpu.VMEM((8, half, model), jnp.float32)] + scratch
        out_shape = [pltpu.VMEM((2, half, model), jnp.bfloat16)] + [pltpu.VMEM((half, model), jnp.bfloat16)] * 2
        out_shape += [pltpu.VMEM((half, model), jnp.float32)] * 4
    else:
        out_shape = [pltpu.VMEM((8, half, model), jnp.float32), pltpu.VMEM((8, 128), jnp.float32)]
    return pl.pallas_call(
        functools.partial(terms_kernel, starts, n, first, last),
        in_specs=in_specs,
        out_specs=[VMEM] * len(out_shape),
        out_shape=out_shape,
        scratch_shapes=scratch,
        input_output_aliases=aliases,
        compiler_params=pltpu.CompilerParams(vmem_limit_bytes=40 << 20),
        cost_estimate=pl.CostEstimate(
            flops=8 * rows * size * model, bytes_accessed=2 * size * model, transcendentals=0
        ),
        name="terms",
    )(*operands)


def input_kernel(place_ref, near, next_pair, two, three, crossed, out, held):
    row, z, x = place_ref[0], place_ref[1], place_ref[2]
    half = two.shape[0]
    pairs = (
        (near.at[0], near.at[1]),
        (next_pair.at[0], next_pair.at[1]),
        (two, crossed.at[0]),
        (three, crossed.at[1]),
    )
    for k, (same, other) in enumerate(pairs):
        slot = 2 * (row ^ z ^ k)
        held[slot + x] = same[...]
        held[slot + (1 - x)] = other[...]
    out[...] = held[...].reshape(8 * half, -1).T


def input_columns(place, near, next_pair, two, three, crossed):
    half, model = two.shape
    return pl.pallas_call(
        input_kernel,
        in_specs=[SMEM] + [VMEM] * 5,
        out_specs=VMEM,
        out_shape=pltpu.VMEM((model, 8 * half), jnp.bfloat16),
        scratch_shapes=[pltpu.VMEM((8, half, model), jnp.bfloat16)],
        compiler_params=pltpu.CompilerParams(vmem_limit_bytes=16 << 20),
        cost_estimate=pl.CostEstimate(flops=0, bytes_accessed=32 * half * model, transcendentals=0),
        name="input_columns",
    )(place, near, next_pair, two, three, crossed)


def outer_kernel(start, offset, size, block, first, place_ref, columns_ref, own, sib, far, *refs):
    out, hidden, tiles, sems = refs if first else refs[1:]
    gather_hidden(place_ref, own, sib, far, start, offset, hidden)
    start = start + offset
    slots = tiles.shape[0]
    copies = []
    for n in range(size // block):
        slot = n % slots
        if n >= slots:
            copies[n - slots].wait()
        tiles[slot] = jnp.dot(
            columns_ref[...], hidden[:, pl.ds(n * block, block)], preferred_element_type=jnp.float32
        ).astype(jnp.bfloat16)
        copies.append(
            pltpu.make_async_copy(tiles.at[slot], out.at[:, pl.ds(start + n * block, block)], sems.at[slot])
        )
        copies[-1].start()
    for copy in copies[-slots:]:
        copy.wait()


def outer_part(place, columns, parts, held, start, offset, size, whole):
    model, tokens = columns.shape
    block = 512
    first = held is None
    vmem, hbm = pl.BlockSpec(memory_space=pltpu.VMEM), pl.BlockSpec(memory_space=pl.ANY)
    operands = [place, columns, *parts] + ([] if first else [held])
    slots = min(3, size // block)
    return pl.pallas_call(
        functools.partial(outer_kernel, start, offset, size, block, first),
        in_specs=[pl.BlockSpec(memory_space=pltpu.SMEM)] + [vmem] * 4 + ([] if first else [hbm]),
        out_specs=hbm,
        out_shape=jax.ShapeDtypeStruct((model, whole), jnp.bfloat16),
        scratch_shapes=[
            pltpu.VMEM((tokens, size), jnp.bfloat16),
            pltpu.VMEM((slots, model, block), jnp.bfloat16),
            pltpu.SemaphoreType.DMA((slots,)),
        ],
        input_output_aliases={} if first else {5: 0},
        compiler_params=pltpu.CompilerParams(vmem_limit_bytes=16 << 20),
        cost_estimate=pl.CostEstimate(
            flops=2 * tokens * size * model, bytes_accessed=2 * size * model, transcendentals=0
        ),
        name="outer",
    )(*operands)


def fenced(value, other):
    return lax.optimization_barrier((value, other))[0]


def swap(value, axis, size, bits):
    return lax.ppermute(value, axis, [(n, n ^ bits) for n in range(size)])


def paired_shards(layer_input, weight, hidden_pre, upstream):
    hidden = hidden_pre.shape[1]
    parts = 2
    sizes = [hidden // parts] * parts
    starts = [sum(sizes[:n]) for n in range(parts)]
    row, col = lax.axis_index("row"), lax.axis_index("col")
    place = jnp.stack([row, col // 2, col % 2, row % 2]).astype(jnp.int32)

    across = functools.partial(swap, axis="col", size=8)
    along = functools.partial(swap, axis="row", size=4)

    *sent, own = hidden_parts(hidden_pre, upstream, starts, sizes)
    sib = along(own, bits=1)
    far = [along(part, bits=2) for part in sent]
    crossed_own = across(fenced(layer_input, own), bits=1)
    two = across(fenced(layer_input, own), bits=4)
    near = pair_of(layer_input, fenced(crossed_own, sib))

    far[0] = fenced(far[0], near)
    pairs = [lax.all_gather(far[0], "row", axis=0, axis_index_groups=CORES)]
    three = across(fenced(layer_input, pairs[0]), bits=6)
    next_pair = across(fenced(near, pairs[0]), bits=2)
    held, token = terms_part(place, [own, fenced(sib, two), pairs[0]], weight, None, starts, sizes, 0)
    joint = pair_of(fenced(two, token), three)
    crossed = across(joint, bits=1)
    far[1], joint, held = lax.optimization_barrier((far[1], joint, held))
    pairs.append(lax.all_gather(far[1], "row", axis=0, axis_index_groups=CORES))
    out = terms_part(place, [own, sib, pairs[1]], weight, held, starts, sizes, 1)
    sends, keeps = out[:3], out[3:]

    arrived = across(sends[0], bits=2)
    got = {k: across(sends[k - 1], bits=1) for k in (2, 3)}
    columns = input_columns(place, near, next_pair, two, three, crossed)
    weight_grad, ends = None, {}
    for n, (m, offset, size) in enumerate(((0, 0, 512), (1, 0, 3072), (0, 512, 2560))):
        weight_grad = outer_part(place, columns, [own, sib, pairs[m]], weight_grad, starts[m], offset, size, hidden)
        if n == 0:
            got[2], weight_grad = lax.optimization_barrier((got[2], weight_grad))
            rounded = (keeps[2] + got[2].astype(jnp.float32)).astype(jnp.bfloat16)
            ends[2] = across(rounded, bits=4)
            columns = fenced(columns, rounded)
        if n == 1:
            got[3], arrived, ends[2], weight_grad = lax.optimization_barrier((got[3], arrived, ends[2], weight_grad))
            rounded = (keeps[3] + got[3].astype(jnp.float32)).astype(jnp.bfloat16)
            ends[3] = across(rounded, bits=6)
            turned = (keeps[1] + arrived[1].astype(jnp.float32)).astype(jnp.bfloat16)
            ends[0] = across(turned, bits=1)
            columns = fenced(columns, (rounded, turned))
    input_sum = keeps[0] + arrived[0].astype(jnp.float32)
    for k in (2, 0, 3):
        input_sum = input_sum + ends[k].astype(jnp.float32)
    return (input_sum.astype(jnp.bfloat16), weight_grad)


def solution(mesh):
    in_specs = (P("col", "row"), P("row", "col"), P("row", "col"), P("row", "col"))
    out_specs = (P("col", "row"), P("row", "col"))
    paired = mesh.shape["row"] == 4 and mesh.shape["col"] == 8
    shards = paired_shards if paired else general_shards
    return jax.shard_map(shards, mesh=mesh, in_specs=in_specs, out_specs=out_specs, check_vma=False)
```

```python
import functools

import jax
import jax.numpy as jnp
from jax import lax
from jax.experimental import pallas as pl
from jax.experimental.pallas import tpu as pltpu
from jax.sharding import PartitionSpec as P

COPIES = 6
VMEM = pl.BlockSpec(memory_space=pltpu.VMEM)
HBM = pl.BlockSpec(memory_space=pltpu.HBM)
SMEM = pl.BlockSpec(memory_space=pltpu.SMEM)


def gelu_slope(value):
    coeff = 0.7978845608028654
    inner = coeff * (value + 0.044715 * value * value * value)
    tanh_val = jnp.tanh(inner)
    return 0.5 * (1.0 + tanh_val) + 0.5 * value * (1.0 - tanh_val * tanh_val) * coeff * (
        1.0 + 3.0 * 0.044715 * value * value
    )


def hidden_grad_of(pre, upstream):
    return (upstream.astype(jnp.float32) * gelu_slope(pre.astype(jnp.float32))).astype(jnp.bfloat16)


def grad_rows(hidden_rows, weight):
    return lax.dot_general(
        hidden_rows, weight, (((1,), (1,)), ((), ())), preferred_element_type=jnp.float32
    )


def outer_sum(input_rows, hidden_rows):
    return lax.dot_general(
        input_rows, hidden_rows, (((0,), (0,)), ((), ())), preferred_element_type=jnp.float32
    )


def general_shards(layer_input, weight, hidden_pre, upstream):
    hidden_grad = hidden_grad_of(hidden_pre, upstream)
    hidden_all = lax.all_gather(hidden_grad, "row", axis=0, tiled=True)
    input_all = lax.all_gather(layer_input, "col", axis=0, tiled=True)
    terms = grad_rows(hidden_all, weight)
    input_sum = lax.psum_scatter(terms, "col", scatter_dimension=0, tiled=True)
    weight_sum = outer_sum(input_all, hidden_all)
    return (input_sum.astype(jnp.bfloat16), weight_sum.astype(jnp.bfloat16))


def slope_columns(pre, up, start, size, outs):
    step = 512

    @pl.loop(0, size // step)
    def _(i):
        here = pl.ds(pl.multiple_of(start + i * step, step), step)
        value = hidden_grad_of(pre[:, here], up[:, here])
        for out, first in outs:
            out[:, pl.ds(pl.multiple_of(first + i * step, step), step)] = value


def hidden_kernel(starts, sizes, pre_hbm, up_hbm, *refs):
    parts, refs = refs[: len(sizes)], refs[len(sizes) :]
    own, pre, up, sems = refs
    copies = []
    for n, (start, size) in enumerate(zip(starts, sizes)):
        cols = pl.ds(start, size)
        for m, (source, target) in enumerate(((pre_hbm, pre), (up_hbm, up))):
            copies.append(pltpu.make_async_copy(source.at[:, cols], target.at[:, cols], sems.at[n, m]))
            copies[-1].start()
    for n, (part, start, size) in enumerate(zip(parts, starts, sizes)):
        copies[2 * n].wait()
        copies[2 * n + 1].wait()
        slope_columns(pre, up, start, size, [(part, 0), (own, start)])


def hidden_parts(pre, up, starts, sizes):
    rows, width = pre.shape
    outs = [(rows, size) for size in sizes] + [(rows, width)]
    return pl.pallas_call(
        functools.partial(hidden_kernel, starts, sizes),
        in_specs=[HBM] * 2,
        out_specs=[VMEM] * len(outs),
        out_shape=[pltpu.VMEM(shape, jnp.bfloat16) for shape in outs],
        scratch_shapes=[
            pltpu.VMEM((rows, width), jnp.bfloat16),
            pltpu.VMEM((rows, width), jnp.bfloat16),
            pltpu.SemaphoreType.DMA((len(sizes), 2)),
        ],
        compiler_params=pltpu.CompilerParams(vmem_limit_bytes=60 << 20),
        cost_estimate=pl.CostEstimate(flops=20 * pre.size, bytes_accessed=6 * pre.size, transcendentals=pre.size),
        name="hidden_grad",
    )(pre, up)


def weight_copies(weight, tiles, sems, start, size):
    rows = weight.shape[0] // COPIES
    return [
        pltpu.make_async_copy(
            weight.at[pl.ds(n * rows, rows), pl.ds(start, size)], tiles.at[pl.ds(n * rows, rows)], sems.at[n]
        )
        for n in range(COPIES)
    ]


def pair_kernel(first, second, out):
    out[0] = first[...]
    out[1] = second[...]


def pair_of(first, second):
    return pl.pallas_call(
        pair_kernel,
        in_specs=[VMEM] * 2,
        out_specs=VMEM,
        out_shape=pltpu.VMEM((2, *first.shape), first.dtype),
        compiler_params=pltpu.CompilerParams(vmem_limit_bytes=16 << 20),
        cost_estimate=pl.CostEstimate(flops=0, bytes_accessed=8 * first.size, transcendentals=0),
        name="pair",
    )(first, second)


def gather_hidden(own, sib, far, farsib, start, offset, hidden):
    rows, size = far.shape[0], hidden.shape[1]
    cols, here = pl.ds(start + offset, size), pl.ds(offset, size)
    for j, part in enumerate((own.at[:, cols], sib.at[:, cols], far.at[:, here], farsib.at[:, here])):
        hidden[pl.ds(rows * j, rows)] = part[...]


def terms_kernel(starts, n, first, last, place_ref, own, sib, far, farsib, weight, *refs):
    held, refs = (None, refs) if first else (refs[0], refs[1:])
    if last:
        sends, keeps, refs = refs[:3], refs[3:7], refs[7:]
        total, hidden, tiles, sems = refs
    else:
        total, hidden, tiles, sems = refs
    copies = weight_copies(weight, tiles, sems, starts[n], tiles.shape[1])
    for copy in copies:
        copy.start()
    gather_hidden(own, sib, far, farsib, starts[n], 0, hidden)
    rows, model = own.shape[0], tiles.shape[0]
    block = model // COPIES
    for i, copy in enumerate(copies):
        copy.wait()
        here = pl.ds(i * block, block)
        term = grad_rows(hidden[...], tiles[here]).reshape(8, rows // 2, block)
        total[:, :, here] = term if first else term + held[:, :, here]

    if last:
        row, z, x = place_ref[0], place_ref[1], place_ref[2]
        slots = [2 * (row ^ z ^ k) for k in range(4)]
        sends[0][0] = total[slots[1] + x].astype(jnp.bfloat16)
        sends[0][1] = total[slots[1] + (1 - x)].astype(jnp.bfloat16)
        for k in (2, 3):
            sends[k - 1][...] = total[slots[k] + (1 - x)].astype(jnp.bfloat16)
            keeps[k][...] = total[slots[k] + x]
        keeps[0][...] = total[slots[0] + x]
        keeps[1][...] = total[slots[0] + (1 - x)]


def terms_part(place, parts, weight, held, starts, sizes, n):
    rows, size = parts[2].shape
    model = weight.shape[0]
    first, last = n == 0, n == len(sizes) - 1
    half = rows // 2
    operands = [place, *parts, weight]
    in_specs = [SMEM] + [VMEM] * 4 + [HBM]
    aliases = {}
    if not first:
        if not last:
            aliases[len(operands)] = 0
        operands.append(held)
        in_specs.append(VMEM)
    scratch = [
        pltpu.VMEM((4 * rows, size), jnp.bfloat16),
        pltpu.VMEM((model, size), jnp.bfloat16),
        pltpu.SemaphoreType.DMA((COPIES,)),
    ]
    if last:
        scratch = [pltpu.VMEM((8, half, model), jnp.float32)] + scratch
        out_shape = [pltpu.VMEM((2, half, model), jnp.bfloat16)] + [pltpu.VMEM((half, model), jnp.bfloat16)] * 2
        out_shape += [pltpu.VMEM((half, model), jnp.float32)] * 4
    else:
        out_shape = [pltpu.VMEM((8, half, model), jnp.float32)]
    return pl.pallas_call(
        functools.partial(terms_kernel, starts, n, first, last),
        in_specs=in_specs,
        out_specs=[VMEM] * len(out_shape),
        out_shape=out_shape,
        scratch_shapes=scratch,
        input_output_aliases=aliases,
        compiler_params=pltpu.CompilerParams(vmem_limit_bytes=40 << 20),
        cost_estimate=pl.CostEstimate(
            flops=8 * rows * size * model, bytes_accessed=2 * size * model, transcendentals=0
        ),
        name="terms",
    )(*operands)


def input_kernel(place_ref, near, next_pair, two, three, crossed, out, held):
    row, z, x = place_ref[0], place_ref[1], place_ref[2]
    half = two.shape[0]
    pairs = (
        (near.at[0], near.at[1]),
        (next_pair.at[0], next_pair.at[1]),
        (two, crossed.at[0]),
        (three, crossed.at[1]),
    )
    for k, (same, other) in enumerate(pairs):
        slot = 2 * (row ^ z ^ k)
        held[slot + x] = same[...]
        held[slot + (1 - x)] = other[...]
    out[...] = held[...].reshape(8 * half, -1).T


def input_columns(place, near, next_pair, two, three, crossed):
    half, model = two.shape
    return pl.pallas_call(
        input_kernel,
        in_specs=[SMEM] + [VMEM] * 5,
        out_specs=VMEM,
        out_shape=pltpu.VMEM((model, 8 * half), jnp.bfloat16),
        scratch_shapes=[pltpu.VMEM((8, half, model), jnp.bfloat16)],
        compiler_params=pltpu.CompilerParams(vmem_limit_bytes=16 << 20),
        cost_estimate=pl.CostEstimate(flops=0, bytes_accessed=32 * half * model, transcendentals=0),
        name="input_columns",
    )(place, near, next_pair, two, three, crossed)


def outer_kernel(start, offset, size, block, first, columns_ref, own, sib, far, farsib, *refs):
    out, hidden, tiles, sems = refs if first else refs[1:]
    gather_hidden(own, sib, far, farsib, start, offset, hidden)
    start = start + offset
    slots = tiles.shape[0]
    copies = []
    for n in range(size // block):
        slot = n % slots
        if n >= slots:
            copies[n - slots].wait()
        tiles[slot] = jnp.dot(
            columns_ref[...], hidden[:, pl.ds(n * block, block)], preferred_element_type=jnp.float32
        ).astype(jnp.bfloat16)
        copies.append(
            pltpu.make_async_copy(tiles.at[slot], out.at[:, pl.ds(start + n * block, block)], sems.at[slot])
        )
        copies[-1].start()
    for copy in copies[-slots:]:
        copy.wait()


def outer_part(columns, parts, held, start, offset, size, whole):
    model, tokens = columns.shape
    block = 512
    first = held is None
    hbm = pl.BlockSpec(memory_space=pl.ANY)
    operands = [columns, *parts] + ([] if first else [held])
    slots = min(3, size // block)
    return pl.pallas_call(
        functools.partial(outer_kernel, start, offset, size, block, first),
        in_specs=[VMEM] * 5 + ([] if first else [hbm]),
        out_specs=hbm,
        out_shape=jax.ShapeDtypeStruct((model, whole), jnp.bfloat16),
        scratch_shapes=[
            pltpu.VMEM((tokens, size), jnp.bfloat16),
            pltpu.VMEM((slots, model, block), jnp.bfloat16),
            pltpu.SemaphoreType.DMA((slots,)),
        ],
        input_output_aliases={} if first else {5: 0},
        compiler_params=pltpu.CompilerParams(vmem_limit_bytes=16 << 20),
        cost_estimate=pl.CostEstimate(
            flops=2 * tokens * size * model, bytes_accessed=2 * size * model, transcendentals=0
        ),
        name="outer",
    )(*operands)


def tied(*values):
    return lax.optimization_barrier(values)


def swap(value, axis, size, bits):
    return lax.ppermute(value, axis, [(n, n ^ bits) for n in range(size)])


def paired_shards(layer_input, weight, hidden_pre, upstream):
    hidden = hidden_pre.shape[1]
    sizes = [hidden // 2] * 2
    starts = [0, hidden // 2]
    row, col = lax.axis_index("row"), lax.axis_index("col")
    place = jnp.stack([row, col // 2, col % 2]).astype(jnp.int32)

    across = functools.partial(swap, axis="col", size=8)
    along = functools.partial(swap, axis="row", size=4)

    *sent, own = hidden_parts(hidden_pre, upstream, starts, sizes)
    sib = along(own, bits=1)
    far = [along(part, bits=2) for part in sent]
    crossed_own, two = across(layer_input, bits=1), across(layer_input, bits=4)
    near = pair_of(layer_input, crossed_own)

    far[0], near, two = tied(far[0], near, two)
    source, far[0] = tied(layer_input, far[0])
    parts = [[own, sib, far[0], along(far[0], bits=1)]]
    three, next_pair = across(source, bits=6), across(near, bits=2)
    held, = terms_part(place, parts[0], weight, None, starts, sizes, 0)
    two, held = tied(two, held)
    joint, far[1] = tied(pair_of(two, three), far[1])
    crossed = across(joint, bits=1)
    parts.append([own, sib, far[1], along(far[1], bits=1)])
    out = terms_part(place, parts[1], weight, held, starts, sizes, 1)
    sends, keeps = out[:3], out[3:]

    arrived = across(sends[0], bits=2)
    got = [across(sends[1], bits=1)]
    columns = input_columns(place, near, next_pair, two, three, crossed)
    small = 512
    weight_grad = outer_part(columns, parts[0], None, starts[0], 0, small, hidden)
    got[0], weight_grad = tied(got[0], weight_grad)
    rounded = (keeps[2] + got[0].astype(jnp.float32)).astype(jnp.bfloat16)
    rounded, weight_grad, late = tied(rounded, weight_grad, sends[2])
    ends = [across(rounded, bits=4)]
    got.append(across(late, bits=1))
    weight_grad = outer_part(columns, parts[1], weight_grad, starts[1], 0, sizes[1], hidden)

    got[1], arrived, ends[0], weight_grad = tied(got[1], arrived, ends[0], weight_grad)
    rounded = (keeps[3] + got[1].astype(jnp.float32)).astype(jnp.bfloat16)
    turned = (keeps[1] + arrived[1].astype(jnp.float32)).astype(jnp.bfloat16)
    rounded, turned, weight_grad = tied(rounded, turned, weight_grad)
    ends += [across(rounded, bits=6), across(turned, bits=1)]
    weight_grad = outer_part(columns, parts[0], weight_grad, starts[0], small, sizes[0] - small, hidden)

    input_sum = keeps[0] + arrived[0].astype(jnp.float32)
    for n in (0, 2, 1):
        input_sum = input_sum + ends[n].astype(jnp.float32)
    return (input_sum.astype(jnp.bfloat16), weight_grad)


def solution(mesh):
    in_specs = (P("col", "row"), P("row", "col"), P("row", "col"), P("row", "col"))
    out_specs = (P("col", "row"), P("row", "col"))
    paired = mesh.shape["row"] == 4 and mesh.shape["col"] == 8
    shards = paired_shards if paired else general_shards
    return jax.shard_map(shards, mesh=mesh, in_specs=in_specs, out_specs=out_specs, check_vma=False)
```

```python
import functools

import jax
import jax.numpy as jnp
from jax import lax
from jax.experimental import pallas as pl
from jax.experimental.pallas import tpu as pltpu
from jax.sharding import PartitionSpec as P

COPIES = 6
VMEM = pl.BlockSpec(memory_space=pltpu.VMEM)
HBM = pl.BlockSpec(memory_space=pltpu.HBM)
SMEM = pl.BlockSpec(memory_space=pltpu.SMEM)


def gelu_slope(value):
    coeff = 0.7978845608028654
    inner = coeff * (value + 0.044715 * value * value * value)
    tanh_val = jnp.tanh(inner)
    return 0.5 * (1.0 + tanh_val) + 0.5 * value * (1.0 - tanh_val * tanh_val) * coeff * (
        1.0 + 3.0 * 0.044715 * value * value
    )


def hidden_grad_of(pre, upstream):
    return (upstream.astype(jnp.float32) * gelu_slope(pre.astype(jnp.float32))).astype(jnp.bfloat16)


def grad_rows(hidden_rows, weight):
    return lax.dot_general(
        hidden_rows, weight, (((1,), (1,)), ((), ())), preferred_element_type=jnp.float32
    )


def outer_sum(input_rows, hidden_rows):
    return lax.dot_general(
        input_rows, hidden_rows, (((0,), (0,)), ((), ())), preferred_element_type=jnp.float32
    )


def general_shards(layer_input, weight, hidden_pre, upstream):
    hidden_grad = hidden_grad_of(hidden_pre, upstream)
    hidden_all = lax.all_gather(hidden_grad, "row", axis=0, tiled=True)
    input_all = lax.all_gather(layer_input, "col", axis=0, tiled=True)
    terms = grad_rows(hidden_all, weight)
    input_sum = lax.psum_scatter(terms, "col", scatter_dimension=0, tiled=True)
    weight_sum = outer_sum(input_all, hidden_all)
    return (input_sum.astype(jnp.bfloat16), weight_sum.astype(jnp.bfloat16))


def slope_columns(pre, up, start, size, outs):
    step = 512

    @pl.loop(0, size // step)
    def _(i):
        here = pl.ds(pl.multiple_of(start + i * step, step), step)
        value = hidden_grad_of(pre[:, here], up[:, here])
        for out, first in outs:
            out[:, pl.ds(pl.multiple_of(first + i * step, step), step)] = value


def hidden_kernel(starts, sizes, pre_hbm, up_hbm, *refs):
    parts, refs = refs[: len(sizes)], refs[len(sizes) :]
    own, pre, up, sems = refs
    copies = []
    for n, (start, size) in enumerate(zip(starts, sizes)):
        cols = pl.ds(start, size)
        for m, (source, target) in enumerate(((pre_hbm, pre), (up_hbm, up))):
            copies.append(pltpu.make_async_copy(source.at[:, cols], target.at[:, cols], sems.at[n, m]))
            copies[-1].start()
    for n, (part, start, size) in enumerate(zip(parts, starts, sizes)):
        copies[2 * n].wait()
        copies[2 * n + 1].wait()
        slope_columns(pre, up, start, size, [(part, 0), (own, start)])


def hidden_parts(pre, up, starts, sizes):
    rows, width = pre.shape
    outs = [(rows, size) for size in sizes] + [(rows, width)]
    return pl.pallas_call(
        functools.partial(hidden_kernel, starts, sizes),
        in_specs=[HBM] * 2,
        out_specs=[VMEM] * len(outs),
        out_shape=[pltpu.VMEM(shape, jnp.bfloat16) for shape in outs],
        scratch_shapes=[
            pltpu.VMEM((rows, width), jnp.bfloat16),
            pltpu.VMEM((rows, width), jnp.bfloat16),
            pltpu.SemaphoreType.DMA((len(sizes), 2)),
        ],
        compiler_params=pltpu.CompilerParams(vmem_limit_bytes=60 << 20),
        cost_estimate=pl.CostEstimate(flops=20 * pre.size, bytes_accessed=6 * pre.size, transcendentals=pre.size),
        name="hidden_grad",
    )(pre, up)


def weight_copies(weight, tiles, sems, start, size):
    rows = weight.shape[0] // COPIES
    return [
        pltpu.make_async_copy(
            weight.at[pl.ds(n * rows, rows), pl.ds(start, size)], tiles.at[pl.ds(n * rows, rows)], sems.at[n]
        )
        for n in range(COPIES)
    ]


def pair_kernel(first, second, out):
    out[0] = first[...]
    out[1] = second[...]


def pair_of(first, second):
    return pl.pallas_call(
        pair_kernel,
        in_specs=[VMEM] * 2,
        out_specs=VMEM,
        out_shape=pltpu.VMEM((2, *first.shape), first.dtype),
        compiler_params=pltpu.CompilerParams(vmem_limit_bytes=16 << 20),
        cost_estimate=pl.CostEstimate(flops=0, bytes_accessed=8 * first.size, transcendentals=0),
        name="pair",
    )(first, second)


def gather_hidden(own, sib, far, farsib, start, offset, hidden):
    rows, size = far.shape[0], hidden.shape[1]
    cols, here = pl.ds(start + offset, size), pl.ds(offset, size)
    for j, part in enumerate((own.at[:, cols], sib.at[:, cols], far.at[:, here], farsib.at[:, here])):
        hidden[pl.ds(rows * j, rows)] = part[...]


def terms_kernel(starts, n, first, last, place_ref, own, sib, far, farsib, weight, *refs):
    held, refs = (None, refs) if first else (refs[0], refs[1:])
    if last:
        sends, keeps, refs = refs[:3], refs[3:7], refs[7:]
        total, hidden, tiles, sems = refs
    else:
        total, hidden, tiles, sems = refs
    copies = weight_copies(weight, tiles, sems, starts[n], tiles.shape[1])
    for copy in copies:
        copy.start()
    gather_hidden(own, sib, far, farsib, starts[n], 0, hidden)
    rows, model = own.shape[0], tiles.shape[0]
    block = model // COPIES
    for i, copy in enumerate(copies):
        copy.wait()
        here = pl.ds(i * block, block)
        term = grad_rows(hidden[...], tiles[here]).reshape(8, rows // 2, block)
        total[:, :, here] = term if first else term + held[:, :, here]

    if last:
        row, z, x = place_ref[0], place_ref[1], place_ref[2]
        slots = [2 * (row ^ z ^ k) for k in range(4)]
        sends[0][0] = total[slots[1] + x].astype(jnp.bfloat16)
        sends[0][1] = total[slots[1] + (1 - x)].astype(jnp.bfloat16)
        for k in (2, 3):
            sends[k - 1][...] = total[slots[k] + (1 - x)].astype(jnp.bfloat16)
            keeps[k][...] = total[slots[k] + x]
        keeps[0][...] = total[slots[0] + x]
        keeps[1][...] = total[slots[0] + (1 - x)]


def terms_part(place, parts, weight, held, starts, sizes, n):
    rows, size = parts[2].shape
    model = weight.shape[0]
    first, last = n == 0, n == len(sizes) - 1
    half = rows // 2
    operands = [place, *parts, weight]
    in_specs = [SMEM] + [VMEM] * 4 + [HBM]
    aliases = {}
    if not first:
        if not last:
            aliases[len(operands)] = 0
        operands.append(held)
        in_specs.append(VMEM)
    scratch = [
        pltpu.VMEM((4 * rows, size), jnp.bfloat16),
        pltpu.VMEM((model, size), jnp.bfloat16),
        pltpu.SemaphoreType.DMA((COPIES,)),
    ]
    if last:
        scratch = [pltpu.VMEM((8, half, model), jnp.float32)] + scratch
        out_shape = [pltpu.VMEM((2, half, model), jnp.bfloat16)] + [pltpu.VMEM((half, model), jnp.bfloat16)] * 2
        out_shape += [pltpu.VMEM((half, model), jnp.float32)] * 4
    else:
        out_shape = [pltpu.VMEM((8, half, model), jnp.float32)]
    return pl.pallas_call(
        functools.partial(terms_kernel, starts, n, first, last),
        in_specs=in_specs,
        out_specs=[VMEM] * len(out_shape),
        out_shape=out_shape,
        scratch_shapes=scratch,
        input_output_aliases=aliases,
        compiler_params=pltpu.CompilerParams(vmem_limit_bytes=40 << 20),
        cost_estimate=pl.CostEstimate(
            flops=8 * rows * size * model, bytes_accessed=2 * size * model, transcendentals=0
        ),
        name="terms",
    )(*operands)


def input_kernel(place_ref, near, next_pair, two, three, crossed, out, held):
    row, z, x = place_ref[0], place_ref[1], place_ref[2]
    half = two.shape[0]
    pairs = (
        (near.at[0], near.at[1]),
        (next_pair.at[0], next_pair.at[1]),
        (two, crossed.at[0]),
        (three, crossed.at[1]),
    )
    for k, (same, other) in enumerate(pairs):
        slot = 2 * (row ^ z ^ k)
        held[slot + x] = same[...]
        held[slot + (1 - x)] = other[...]
    out[...] = held[...].reshape(8 * half, -1).T


def input_columns(place, near, next_pair, two, three, crossed):
    half, model = two.shape
    return pl.pallas_call(
        input_kernel,
        in_specs=[SMEM] + [VMEM] * 5,
        out_specs=VMEM,
        out_shape=pltpu.VMEM((model, 8 * half), jnp.bfloat16),
        scratch_shapes=[pltpu.VMEM((8, half, model), jnp.bfloat16)],
        compiler_params=pltpu.CompilerParams(vmem_limit_bytes=16 << 20),
        cost_estimate=pl.CostEstimate(flops=0, bytes_accessed=32 * half * model, transcendentals=0),
        name="input_columns",
    )(place, near, next_pair, two, three, crossed)


def outer_kernel(start, offset, size, block, first, columns_ref, own, sib, far, farsib, *refs):
    out, hidden, tiles, sems = refs if first else refs[1:]
    gather_hidden(own, sib, far, farsib, start, offset, hidden)
    start = start + offset
    slots = tiles.shape[0]
    copies = []
    for n in range(size // block):
        slot = n % slots
        if n >= slots:
            copies[n - slots].wait()
        tiles[slot] = jnp.dot(
            columns_ref[...], hidden[:, pl.ds(n * block, block)], preferred_element_type=jnp.float32
        ).astype(jnp.bfloat16)
        copies.append(
            pltpu.make_async_copy(tiles.at[slot], out.at[:, pl.ds(start + n * block, block)], sems.at[slot])
        )
        copies[-1].start()
    for copy in copies[-slots:]:
        copy.wait()


def outer_part(columns, parts, held, start, offset, size, whole):
    model, tokens = columns.shape
    block = 512
    first = held is None
    hbm = pl.BlockSpec(memory_space=pl.ANY)
    operands = [columns, *parts] + ([] if first else [held])
    slots = min(3, size // block)
    return pl.pallas_call(
        functools.partial(outer_kernel, start, offset, size, block, first),
        in_specs=[VMEM] * 5 + ([] if first else [hbm]),
        out_specs=hbm,
        out_shape=jax.ShapeDtypeStruct((model, whole), jnp.bfloat16),
        scratch_shapes=[
            pltpu.VMEM((tokens, size), jnp.bfloat16),
            pltpu.VMEM((slots, model, block), jnp.bfloat16),
            pltpu.SemaphoreType.DMA((slots,)),
        ],
        input_output_aliases={} if first else {5: 0},
        compiler_params=pltpu.CompilerParams(vmem_limit_bytes=16 << 20),
        cost_estimate=pl.CostEstimate(
            flops=2 * tokens * size * model, bytes_accessed=2 * size * model, transcendentals=0
        ),
        name="outer",
    )(*operands)


def tied(*values):
    return lax.optimization_barrier(values)


def swap(value, axis, size, bits):
    return lax.ppermute(value, axis, [(n, n ^ bits) for n in range(size)])


def paired_shards(layer_input, weight, hidden_pre, upstream):
    hidden = hidden_pre.shape[1]
    sizes = [hidden // 2] * 2
    starts = [0, hidden // 2]
    row, col = lax.axis_index("row"), lax.axis_index("col")
    place = jnp.stack([row, col // 2, col % 2]).astype(jnp.int32)

    across = functools.partial(swap, axis="col", size=8)
    along = functools.partial(swap, axis="row", size=4)

    *sent, own = hidden_parts(hidden_pre, upstream, starts, sizes)
    far = [along(part, bits=2) for part in sent]
    crossed_own, two = across(layer_input, bits=1), across(layer_input, bits=4)
    crossed_own, two = tied(crossed_own, two)
    own, near = tied(own, pair_of(layer_input, crossed_own))
    sib = along(own, bits=1)

    far[0], near = tied(far[0], near)
    source, far[0] = tied(layer_input, far[0])
    parts = [[own, sib, far[0], along(far[0], bits=1)]]
    three, next_pair = across(source, bits=6), across(near, bits=2)
    held, = terms_part(place, parts[0], weight, None, starts, sizes, 0)
    two, held = tied(two, held)
    joint, far[1] = tied(pair_of(two, three), far[1])
    crossed = across(joint, bits=1)
    parts.append([own, sib, far[1], along(far[1], bits=1)])
    out = terms_part(place, parts[1], weight, held, starts, sizes, 1)
    sends, keeps = out[:3], out[3:]

    arrived = across(sends[0], bits=2)
    got = [across(sends[1], bits=1)]
    columns = input_columns(place, near, next_pair, two, three, crossed)
    small = 512
    weight_grad = outer_part(columns, parts[0], None, starts[0], 0, small, hidden)
    got[0], weight_grad = tied(got[0], weight_grad)
    rounded = (keeps[2] + got[0].astype(jnp.float32)).astype(jnp.bfloat16)
    rounded, weight_grad, late = tied(rounded, weight_grad, sends[2])
    ends = [across(rounded, bits=4)]
    got.append(across(late, bits=1))
    weight_grad = outer_part(columns, parts[1], weight_grad, starts[1], 0, sizes[1], hidden)

    got[1], arrived, ends[0], weight_grad = tied(got[1], arrived, ends[0], weight_grad)
    rounded = (keeps[3] + got[1].astype(jnp.float32)).astype(jnp.bfloat16)
    turned = (keeps[1] + arrived[1].astype(jnp.float32)).astype(jnp.bfloat16)
    rounded, turned, weight_grad = tied(rounded, turned, weight_grad)
    ends += [across(rounded, bits=6), across(turned, bits=1)]
    weight_grad = outer_part(columns, parts[0], weight_grad, starts[0], small, sizes[0] - small, hidden)

    input_sum = keeps[0] + arrived[0].astype(jnp.float32)
    for n in (0, 2, 1):
        input_sum = input_sum + ends[n].astype(jnp.float32)
    return (input_sum.astype(jnp.bfloat16), weight_grad)


def solution(mesh):
    in_specs = (P("col", "row"), P("row", "col"), P("row", "col"), P("row", "col"))
    out_specs = (P("col", "row"), P("row", "col"))
    paired = mesh.shape["row"] == 4 and mesh.shape["col"] == 8
    shards = paired_shards if paired else general_shards
    return jax.shard_map(shards, mesh=mesh, in_specs=in_specs, out_specs=out_specs, check_vma=False)
```
